32 devices in a mesh: chan: 8 (over y, x, core), freq: 4 (over z), win: 1.
Axes of the slice: x: 2, y: 2, z: 4, core: 2. Of those that a mesh axis runs over, the one named last changes fastest.
Arguments:
- rec_block: bfloat16 [12, 32, 6000], P('win', ('chan', 'freq')), may hold values from -70 to 70
- rec_partner: bfloat16 [12, 128, 6000], P('win', ('chan', 'freq')), may hold values from -70 to 70
- flag_block: int32 [12, 32], P('win', ('chan', 'freq')), may hold values 0 or 1
- flag_partner: int32 [12, 128], P('win', ('chan', 'freq')), may hold values 0 or 1
Outputs:
- cross: float32 [2, 512, 32, 128], P(None, 'freq', 'chan', 'win')
The draws below stay inside these ranges and needn't reach their ends.
All inputs are finite; a program needn't handle non-finite values. No bound on the sum of `flag_block` or of `flag_partner` on one device may be relied on, other than what follows from the above.
Results may differ from the reference program's by a relative error of at most 0.0059.
Values may be sent and summed in bfloat16 or wider, within the bound.
A program may use at most 64 MiB of HBM per device.

```python
import math
import jax
import jax.numpy as jnp
from jax import lax

SEGMENT_READINGS = 6000
F = 512
FLO = 60
NWIN = 12
CA = 32
CB = 128


def tone_field(key, noise, spread):
    windows, rows, reading_offsets = noise.shape
    keys = jax.random.split(key, 4)
    pure_signal_slot = jax.random.randint(keys[0], (windows, rows, 1), 0, reading_offsets // 4)
    initial_offset = jax.random.uniform(keys[1], (windows, rows, 1), minval=-math.pi, maxval=math.pi)
    strength = jnp.exp(jax.random.uniform(keys[2], (windows, rows, 1), minval=math.log(0.1), maxval=0.0))
    amplitude = 2.0 * jnp.sqrt(strength * F / reading_offsets)
    channel_gain = jnp.exp(jax.random.uniform(keys[3], (windows, rows, 1), minval=0.0, maxval=math.log(spread)))
    reading_moments = jnp.arange(reading_offsets, dtype=jnp.int32)
    cycle_radians = (pure_signal_slot * reading_moments % reading_offsets).astype(jnp.float32) * (2.0 * math.pi / reading_offsets) + initial_offset
    return (channel_gain * (noise + amplitude * jnp.cos(cycle_radians))).astype(jnp.bfloat16)


def draw_rec_block(key, part):
    key = jax.random.fold_in(key, 11)
    key_noise, key_rest = jax.random.split(key)
    shape = (NWIN, CA, SEGMENT_READINGS)
    noise = jax.random.truncated_normal(key_noise, -6.0, 6.0, shape)
    return tone_field(key_rest, noise, 10.0)


def draw_rec_partner(key, part):
    key = jax.random.fold_in(key, 23)
    key_noise, key_rest = jax.random.split(key)
    shape = (NWIN, CB, SEGMENT_READINGS)
    noise = jax.random.truncated_normal(key_noise, -6.0, 6.0, shape)
    return tone_field(key_rest, noise, 10.0)


def plant(drawn, own_key, low, top_value):
    longest = drawn.shape.index(max(drawn.shape))
    spots = []
    for shift in (0, 1):
        where = [jax.random.randint(jax.random.fold_in(own_key, axis), (), 0, length) for axis, length in enumerate(drawn.shape)]
        where[longest] = (where[longest] + shift) % drawn.shape[longest]
        spots.append(tuple(where))
    return drawn.at[spots[0]].set(low).at[spots[1]].set(top_value)


def setup_inputs(seed: int = 0) -> dict:
    key_of = jax.random.split(jax.random.key(seed), 5)
    rec_block = draw_rec_block(jax.random.fold_in(key_of[4], 71), 0)
    rec_partner = draw_rec_partner(jax.random.fold_in(key_of[4], 71), 0)
    flag_block = plant((jax.random.randint(key_of[2], (NWIN, CA), 0, 8) < 7).astype(jnp.int32), jax.random.fold_in(key_of[2], 1), 0, 1)
    flag_partner = plant((jax.random.randint(key_of[3], (NWIN, CB), 0, 8) < 7).astype(jnp.int32), jax.random.fold_in(key_of[3], 1), 0, 1)
    return {"rec_block": rec_block, "rec_partner": rec_partner, "flag_block": flag_block, "flag_partner": flag_partner}


def harmonic_kernel_grid(reading_moments, spectral_slots, reading_offsets):
    cycle_offset = reading_moments[:, None] * spectral_slots[None, :] % reading_offsets
    cycle_radians = cycle_offset.astype(jnp.float32) * (2.0 * math.pi / reading_offsets)
    return jnp.concatenate([jnp.cos(cycle_radians), -jnp.sin(cycle_radians)], axis=1).astype(jnp.bfloat16)

def whiten(records, quality, harmonic_operator):

    def per_window(window_rec):
        return jnp.dot(window_rec, harmonic_operator, preferred_element_type=jnp.float32)
    spectra = lax.map(per_window, records)
    spectra = spectra.reshape(records.shape[0], records.shape[1], 2, F)
    band_power = lax.optimization_barrier(jnp.sum(spectra * spectra, axis=(2, 3), keepdims=True)) / F
    weights = quality.astype(jnp.float32)[:, :, None, None]
    whitened = (weights * spectra * lax.rsqrt(band_power + 1e-06)).astype(jnp.bfloat16)
    return jnp.transpose(whitened, (0, 2, 1, 3))

def reference(rec_block, rec_partner, flag_block, flag_partner):
    reading_moments = jnp.arange(SEGMENT_READINGS, dtype=jnp.int32)
    spectral_slots = jnp.arange(F, dtype=jnp.int32) + FLO
    harmonic_operator = harmonic_kernel_grid(reading_moments, spectral_slots, SEGMENT_READINGS)
    white_block = whiten(rec_block, flag_block, harmonic_operator).astype(jnp.float32)
    white_partner = whiten(rec_partner, flag_partner, harmonic_operator).astype(jnp.float32)
    turned = jnp.concatenate([white_block[:, 1:2], -white_block[:, 0:1]], axis=1)
    paired = jnp.stack([white_block, turned])
    summed = jnp.einsum('owsaf,wsbf->ofab', paired, white_partner, precision=lax.Precision.HIGHEST)
    return summed * (1.0 / math.sqrt(NWIN))
```

```python
import functools
import math

import jax
import jax.numpy as jnp
import ml_dtypes
import numpy as np
from jax import lax
from jax.experimental import pallas as pl
from jax.experimental.pallas import tpu as pltpu
from jax.sharding import PartitionSpec as P

F = 512
FLO = 60


def harmonic_kernel_grid(reading_moments, spectral_slots, reading_offsets):
    cycle_offset = reading_moments[:, None] * spectral_slots[None, :] % reading_offsets
    cycle_radians = cycle_offset.astype(jnp.float32) * (2.0 * math.pi / reading_offsets)
    return jnp.concatenate([jnp.cos(cycle_radians), -jnp.sin(cycle_radians)], axis=1).astype(
        jnp.bfloat16
    )


def transform(records):
    reading_offsets = records.shape[1]
    extent_count = reading_offsets // 4
    spectral_slots = jnp.arange(F, dtype=jnp.int32) + FLO
    accumulated = jnp.zeros((records.shape[0], 2 * F), jnp.float32)
    for cosine_lag in range(4):
        reading_moments = jnp.arange(extent_count, dtype=jnp.int32) + cosine_lag * extent_count
        harmonic_operator = harmonic_kernel_grid(reading_moments, spectral_slots, reading_offsets)
        accumulated = accumulated + jnp.dot(
            records[:, cosine_lag * extent_count : (cosine_lag + 1) * extent_count],
            harmonic_operator,
            preferred_element_type=jnp.float32,
        )
    return accumulated


def rotate(whitened):
    turned = jnp.concatenate([whitened[:, 1:2], -whitened[:, 0:1]], axis=1)
    return jnp.stack([whitened, turned])


def body(rec_block, rec_partner, flag_block, flag_partner):
    windows, block_dev, reading_offsets = rec_block.shape
    partner_dev = rec_partner.shape[1]
    channels = block_dev + partner_dev
    records = jnp.concatenate([rec_block, rec_partner], axis=1).reshape(
        windows * channels, reading_offsets
    )
    spectra = transform(records).reshape(windows, channels, 2, F)
    band_power = jnp.sum(spectra * spectra, axis=(2, 3), keepdims=True) / F
    quality = jnp.concatenate([flag_block, flag_partner], axis=1).astype(jnp.float32)[
        :, :, None, None
    ]
    whitened = (quality * spectra * lax.rsqrt(band_power + 1e-06)).astype(jnp.bfloat16)
    whitened = jnp.transpose(whitened, (0, 2, 1, 3))
    block_white = whitened[:, :, :block_dev]
    partner_white = whitened[:, :, block_dev:]
    block_white, partner_white = (
        lax.all_to_all(block_white, "freq", split_axis=3, concat_axis=2, tiled=True),
        lax.all_to_all(partner_white, "freq", split_axis=3, concat_axis=2, tiled=True),
    )
    stack_scale = 1.0 / math.sqrt(windows * lax.axis_size("win"))
    paired = rotate(block_white)
    partials = jnp.einsum(
        "owsaf,wsbf->ofab",
        paired,
        lax.all_gather(partner_white, "chan", axis=2, tiled=True),
        preferred_element_type=jnp.float32,
    )
    summed = lax.psum_scatter(partials, "win", scatter_dimension=3, tiled=True)
    return summed * stack_scale


MESH = pl.DeviceIdType.MESH
LANES = 128
DIRECT = (1, 2, 4, 6)


def basis_table(samples):
    s = np.arange(samples, dtype=np.int64)[:, None]
    k = np.arange(F, dtype=np.int64)[None, :] + FLO
    phase = (s * k % samples).astype(np.float64) * (2.0 * np.pi / samples)
    return np.concatenate([np.cos(phase), -np.sin(phase)], axis=1).astype(ml_dtypes.bfloat16)


def flip(chan, d):
    core, x, y = chan % 2, (chan // 2) % 2, chan // 4
    core = 1 - core if d & 1 else core
    x = 1 - x if d & 2 else x
    y = 1 - y if d & 4 else y
    return core + 2 * x + 4 * y


def kernel(
    chunks, scale,
    blk_hbm, par_hbm, fb_ref, fp_ref, basis_hbm, out_ref,
    blk, par, basis, xs, slabs, zbuf, gath, coef, res,
    load_sem, basis_sem, z_send, z_recv, p_send, p_recv,
):
    chan, z, win = lax.axis_index("chan"), lax.axis_index("freq"), lax.axis_index("win")
    nwin = blk.shape[0]

    blk_in = pltpu.make_async_copy(blk_hbm, blk, load_sem.at[0])
    par_in = pltpu.make_async_copy(par_hbm, par, load_sem.at[1])
    blk_in.start()
    par_in.start()
    loads = []
    for i, (low, size) in enumerate(chunks):
        rows = pl.ds(low, size)
        load = pltpu.make_async_copy(basis_hbm.at[rows], basis.at[rows], basis_sem.at[i])
        load.start()
        loads.append(load)

    barrier = pltpu.get_barrier_semaphore()
    for r in (1, 2, 3):
        pl.semaphore_signal(barrier, inc=1, device_id=(chan, (z + r) % 4, win), device_id_type=MESH)
    for d in DIRECT:
        pl.semaphore_signal(barrier, inc=1, device_id=(flip(chan, d), z, win), device_id_type=MESH)

    par_in.wait()
    for w in range(nwin):
        xs[w * 4 : w * 4 + 4, :] = par[w].astype(jnp.float32)
    blk_in.wait()
    top = nwin * 4
    xs[top : top + nwin, :] = blk[...].astype(jnp.float32)
    xs[top + nwin :, :] = jnp.zeros((xs.shape[0] - top - nwin, xs.shape[1]), jnp.float32)

    spec = None
    for load, (low, size) in zip(loads, chunks):
        load.wait()
        x = xs[:, low : low + size].astype(jnp.bfloat16)
        term = jnp.dot(x, basis[low : low + size, :], preferred_element_type=jnp.float32)
        spec = term if spec is None else spec + term

    power = jnp.sum(spec * spec, axis=1, keepdims=True) * (1.0 / F)
    quality = jnp.concatenate([fp_ref[...], fb_ref[...]], axis=0).astype(jnp.float32)
    quality = jnp.concatenate(
        [quality, jnp.zeros((xs.shape[0] - top - nwin, 1), jnp.float32)], axis=0
    )
    white = quality * spec * lax.rsqrt(power + 1e-06)

    upper = lax.broadcasted_iota(jnp.int32, (8, LANES), 0) < 4
    for k in range(4):
        re = white[:, k * LANES : (k + 1) * LANES]
        im = white[:, F + k * LANES : F + (k + 1) * LANES]
        pieces = []
        for pair in range(nwin // 2):
            re_p, im_p = re[pair * 8 : pair * 8 + 8], im[pair * 8 : pair * 8 + 8]
            pieces.append(jnp.where(upper, re_p, pltpu.roll(im_p, 4, 0)))
            pieces.append(jnp.where(upper, pltpu.roll(re_p, 4, 0), im_p))
        pieces.append(re[top : top + 16])
        pieces.append(im[top : top + 16])
        slabs[k] = jnp.concatenate(pieces, axis=0).astype(jnp.bfloat16)
    zbuf[z] = slabs[z]

    def z_copy(r):
        return pltpu.make_async_remote_copy(
            src_ref=slabs.at[(z + r) % 4], dst_ref=zbuf.at[z],
            send_sem=z_send.at[r - 1], recv_sem=z_recv.at[r - 1],
            device_id=(chan, (z + r) % 4, win), device_id_type=MESH,
        )

    used = pl.ds(0, nwin * 8)

    def plane_copy(d, r):
        slot = (z + 4 - r) % 4
        return pltpu.make_async_remote_copy(
            src_ref=zbuf.at[slot, used], dst_ref=gath.at[d, slot],
            send_sem=p_send.at[d, r], recv_sem=p_recv.at[d, r],
            device_id=(flip(chan, d), z, win), device_id_type=MESH,
        )

    def relay_copy(d, r):
        slot = (z + 4 - r) % 4
        return pltpu.make_async_remote_copy(
            src_ref=gath.at[d, slot], dst_ref=gath.at[d + 1, slot],
            send_sem=p_send.at[d + 1, r], recv_sem=p_recv.at[d + 1, r],
            device_id=(flip(chan, 1), z, win), device_id_type=MESH,
        )

    pl.semaphore_wait(barrier, 3 + len(DIRECT))
    for r in (1, 3, 2):
        z_copy(r).start()
    for d in (6, 2, 4, 1):
        plane_copy(d, 0).start()
    last = None
    for r in (1, 3, 2):
        z_copy(r).wait_recv()
        for d in (6, 2, 4, 1):
            plane_copy(d, r).start()

    for a in range(4):
        tail = zbuf[a, top * 2 : top * 2 + 32].astype(jnp.float32) * scale
        for w in range(nwin):
            re_a = jnp.broadcast_to(tail[w : w + 1], (8, LANES))
            im_a = jnp.broadcast_to(tail[16 + w : 17 + w], (8, LANES))
            coef[0, a, w] = jnp.where(upper, re_a, im_a)
            coef[1, a, w] = jnp.where(upper, im_a, -re_a)

    for r in (0, 1, 3, 2):
        for d in (2, 4, 6):
            plane_copy(d, r).wait_recv()
            relay_copy(d, r).start()

    def block(read, first):
        def pair_step(pair, carry):
            b0 = read(pair * 2).astype(jnp.float32).reshape(nwin, 8, LANES)
            b1 = read(pair * 2 + 1).astype(jnp.float32).reshape(nwin, 8, LANES)
            for o in range(2):
                for a in range(4):
                    c = coef[o, a]
                    p0 = jnp.sum(c * b0, axis=0)
                    p1 = jnp.sum(c * b1, axis=0)
                    p0 = p0 + pltpu.roll(p0, 4, 0)
                    p1 = p1 + pltpu.roll(p1, 4, 0)
                    start = pl.multiple_of(first + pair * 8, 8)
                    res[o, a, pl.ds(start, 8), :] = jnp.where(upper, p0, p1)
            return carry

        lax.fori_loop(0, 2, pair_step, 0)

    block(lambda k: zbuf[k, 0 : nwin * 8], chan * 16)
    for d in (2, 4, 6, 1, 3, 5, 7):
        if d not in DIRECT:
            for r in range(4):
                relay_copy(d - 1, r).wait_recv()
        elif d == 1:
            for r in range(4):
                plane_copy(d, r).wait_recv()
        block(lambda k, d=d: gath[d, k], flip(chan, d) * 16)

    for o in range(2):
        for a in range(4):
            out_ref[o, :, a, :] = res[o, a].T

    for r in (1, 2, 3):
        z_copy(r).wait_send()
    for r in range(4):
        for d in DIRECT:
            plane_copy(d, r).wait_send()
        for d in (2, 4, 6):
            relay_copy(d, r).wait_send()


def fused_body(rec_block, rec_partner, flag_block, flag_partner):
    nwin, _, samples = rec_block.shape
    step = 1536
    chunks = [(low, min(step, samples - low)) for low in range(0, samples, step)]
    basis = jnp.asarray(basis_table(samples))
    vmem = pl.BlockSpec(memory_space=pltpu.VMEM)
    hbm = pl.BlockSpec(memory_space=pl.ANY)
    rows = nwin * 4 + 16
    return pl.pallas_call(
        functools.partial(kernel, chunks, 1.0 / math.sqrt(nwin)),
        out_shape=jax.ShapeDtypeStruct((2, LANES, 4, LANES), jnp.float32),
        in_specs=[hbm, hbm, vmem, vmem, hbm],
        out_specs=vmem,
        scratch_shapes=[
            pltpu.VMEM((nwin, samples), jnp.bfloat16),
            pltpu.VMEM((nwin, 4, samples), jnp.bfloat16),
            pltpu.VMEM((samples, 2 * F), jnp.bfloat16),
            pltpu.VMEM((rows, samples), jnp.float32),
            pltpu.VMEM((4, nwin * 8 + 32, LANES), jnp.bfloat16),
            pltpu.VMEM((4, nwin * 8 + 32, LANES), jnp.bfloat16),
            pltpu.VMEM((8, 4, nwin * 8, LANES), jnp.bfloat16),
            pltpu.VMEM((2, 4, nwin, 8, LANES), jnp.float32),
            pltpu.VMEM((2, 4, LANES, LANES), jnp.float32),
            pltpu.SemaphoreType.DMA((2,)),
            pltpu.SemaphoreType.DMA((len(chunks),)),
            pltpu.SemaphoreType.DMA((3,)),
            pltpu.SemaphoreType.DMA((3,)),
            pltpu.SemaphoreType.DMA((8, 4)),
            pltpu.SemaphoreType.DMA((8, 4)),
        ],
        compiler_params=pltpu.CompilerParams(
            collective_id=0, has_side_effects=True, vmem_limit_bytes=40 * 1024 * 1024
        ),
    )(
        rec_block.reshape(nwin, samples),
        rec_partner,
        flag_block.reshape(nwin, 1),
        flag_partner.reshape(nwin * 4, 1),
        basis,
    )


def solution(mesh):
    placed = (
        P("win", ("chan", "freq"), None),
        P("win", ("chan", "freq"), None),
        P("win", ("chan", "freq")),
        P("win", ("chan", "freq")),
    )
    small = dict(mesh.shape) == {"chan": 8, "freq": 4, "win": 1}
    return jax.shard_map(
        fused_body if small else body,
        mesh=mesh,
        in_specs=placed,
        out_specs=P(None, "freq", "chan", "win"),
        check_vma=False,
    )
```

```python
import functools
import math

import jax
import jax.numpy as jnp
import ml_dtypes
import numpy as np
from jax import lax
from jax.experimental import pallas as pl
from jax.experimental.pallas import tpu as pltpu
from jax.sharding import PartitionSpec as P

F = 512
FLO = 60


def harmonic_kernel_grid(reading_moments, spectral_slots, reading_offsets):
    cycle_offset = reading_moments[:, None] * spectral_slots[None, :] % reading_offsets
    cycle_radians = cycle_offset.astype(jnp.float32) * (2.0 * math.pi / reading_offsets)
    return jnp.concatenate([jnp.cos(cycle_radians), -jnp.sin(cycle_radians)], axis=1).astype(
        jnp.bfloat16
    )


def transform(records):
    reading_offsets = records.shape[1]
    extent_count = reading_offsets // 4
    spectral_slots = jnp.arange(F, dtype=jnp.int32) + FLO
    accumulated = jnp.zeros((records.shape[0], 2 * F), jnp.float32)
    for cosine_lag in range(4):
        reading_moments = jnp.arange(extent_count, dtype=jnp.int32) + cosine_lag * extent_count
        harmonic_operator = harmonic_kernel_grid(reading_moments, spectral_slots, reading_offsets)
        accumulated = accumulated + jnp.dot(
            records[:, cosine_lag * extent_count : (cosine_lag + 1) * extent_count],
            harmonic_operator,
            preferred_element_type=jnp.float32,
        )
    return accumulated


def rotate(whitened):
    turned = jnp.concatenate([whitened[:, 1:2], -whitened[:, 0:1]], axis=1)
    return jnp.stack([whitened, turned])


def body(rec_block, rec_partner, flag_block, flag_partner):
    windows, block_dev, reading_offsets = rec_block.shape
    partner_dev = rec_partner.shape[1]
    channels = block_dev + partner_dev
    records = jnp.concatenate([rec_block, rec_partner], axis=1).reshape(
        windows * channels, reading_offsets
    )
    spectra = transform(records).reshape(windows, channels, 2, F)
    band_power = jnp.sum(spectra * spectra, axis=(2, 3), keepdims=True) / F
    quality = jnp.concatenate([flag_block, flag_partner], axis=1).astype(jnp.float32)[
        :, :, None, None
    ]
    whitened = (quality * spectra * lax.rsqrt(band_power + 1e-06)).astype(jnp.bfloat16)
    whitened = jnp.transpose(whitened, (0, 2, 1, 3))
    block_white = whitened[:, :, :block_dev]
    partner_white = whitened[:, :, block_dev:]
    block_white, partner_white = (
        lax.all_to_all(block_white, "freq", split_axis=3, concat_axis=2, tiled=True),
        lax.all_to_all(partner_white, "freq", split_axis=3, concat_axis=2, tiled=True),
    )
    stack_scale = 1.0 / math.sqrt(windows * lax.axis_size("win"))
    paired = rotate(block_white)
    partials = jnp.einsum(
        "owsaf,wsbf->ofab",
        paired,
        lax.all_gather(partner_white, "chan", axis=2, tiled=True),
        preferred_element_type=jnp.float32,
    )
    summed = lax.psum_scatter(partials, "win", scatter_dimension=3, tiled=True)
    return summed * stack_scale


MESH = pl.DeviceIdType.MESH
LANES = 128
DIRECT = (1, 2, 4, 6)


def basis_table(samples, depth):
    r = np.arange(samples // 4, dtype=np.int64)[:, None]
    lane = np.arange(LANES)
    table = np.zeros((depth, 4, 2, LANES), np.float64)
    for m in range(4):
        slab = (lane // 32 - m) % 4
        k = FLO + slab * LANES + 4 * (lane % 32) + (m - FLO) % 4
        phase = (r * k[None, :] % samples).astype(np.float64) * (2.0 * np.pi / samples)
        table[: samples // 4, m, 0] = np.cos(phase)
        table[: samples // 4, m, 1] = -np.sin(phase)
    return table.reshape(depth, 8 * LANES).astype(ml_dtypes.bfloat16)


def split(value):
    high = value.astype(jnp.bfloat16)
    return high, (value - high.astype(jnp.float32)).astype(jnp.bfloat16)


def flip(chan, d):
    core, x, y = chan % 2, (chan // 2) % 2, chan // 4
    core = 1 - core if d & 1 else core
    x = 1 - x if d & 2 else x
    y = 1 - y if d & 4 else y
    return core + 2 * x + 4 * y


def kernel(
    samples, scale,
    blk_hbm, par_hbm, fb_ref, fp_ref, basis_hbm, out_ref,
    blk, par, basis, xs, slabs, zbuf, gath, coef, res,
    load_sem, basis_sem, z_send, z_recv, p_send, p_recv,
):
    chan, z, win = lax.axis_index("chan"), lax.axis_index("freq"), lax.axis_index("win")
    nwin = blk.shape[0]

    blk_in = pltpu.make_async_copy(blk_hbm, blk, load_sem.at[0])
    par_in = pltpu.make_async_copy(par_hbm, par, load_sem.at[1])
    blk_in.start()
    par_in.start()
    basis_in = pltpu.make_async_copy(basis_hbm, basis, basis_sem)
    basis_in.start()

    barrier = pltpu.get_barrier_semaphore()
    for r in (1, 2, 3):
        pl.semaphore_signal(barrier, inc=1, device_id=(chan, (z + r) % 4, win), device_id_type=MESH)
    for d in DIRECT:
        pl.semaphore_signal(barrier, inc=1, device_id=(flip(chan, d), z, win), device_id_type=MESH)

    rows = xs.shape[0]
    top = nwin * 4
    edge = samples // LANES * LANES
    xs[:, edge:] = jnp.zeros((rows, xs.shape[1] - edge), jnp.float32)
    xs[top + nwin :, :] = jnp.zeros((rows - top - nwin, xs.shape[1]), jnp.float32)
    par_in.wait()
    for w in range(nwin):
        xs[w * 4 : w * 4 + 4, 0:samples] = par[w].astype(jnp.float32)
    blk_in.wait()
    xs[top : top + nwin, 0:samples] = blk[...].astype(jnp.float32)

    quarter, depth = samples // 4, basis.shape[0]
    x0, x1, x2, x3 = (xs[:, q * quarter : q * quarter + depth] for q in range(4))
    even, odd = x0 + x2, x1 + x3
    a_hi, a_lo = split(x0 - x2)
    b_hi, b_lo = split(x1 - x3)
    sum_hi, sum_lo = split(even + odd)
    alt_hi, alt_lo = split(even - odd)
    basis_in.wait()

    def transform_rows(parts, m):
        return jnp.dot(
            jnp.concatenate(parts, axis=0),
            basis[:, m * 2 * LANES : (m + 1) * 2 * LANES],
            preferred_element_type=jnp.float32,
        )

    spec_re, spec_im = [], []
    for m in range(4):
        if m % 2 == 0:
            got = transform_rows([sum_hi, sum_lo] if m == 0 else [alt_hi, alt_lo], m)
            got = got[:rows] + got[rows:]
            re, im = got[:, :LANES], got[:, LANES:]
        else:
            got = transform_rows([a_hi, a_lo, b_hi, b_lo], m)
            a = got[:rows] + got[rows : 2 * rows]
            b = got[2 * rows : 3 * rows] + got[3 * rows :]
            sign = 1.0 if m == 1 else -1.0
            re = a[:, :LANES] + sign * b[:, LANES:]
            im = a[:, LANES:] - sign * b[:, :LANES]
        spec_re.append(re)
        spec_im.append(im)

    power = sum(re * re + im * im for re, im in zip(spec_re, spec_im))
    power = jnp.sum(power, axis=1, keepdims=True) * (1.0 / F)
    row = lax.broadcasted_iota(jnp.int32, (rows, nwin), 0)
    lane = lax.broadcasted_iota(jnp.int32, (rows, nwin), 1)
    flags = jnp.concatenate(
        [fp_ref[...].astype(jnp.float32)] * nwin
        + [jnp.broadcast_to(fb_ref[...].astype(jnp.float32), (rows - top, nwin))],
        axis=0,
    )
    window = jnp.where(row < top, row // 4, row - top)
    quality = jnp.sum(jnp.where(lane == window, flags, 0.0), axis=1, keepdims=True)
    weight = quality * lax.rsqrt(power + 1e-06)

    upper = lax.broadcasted_iota(jnp.int32, (8, LANES), 0) < 4
    group = lax.broadcasted_iota(jnp.int32, (rows, LANES), 1) // 32
    for k in range(4):
        re, im = spec_re[(3 - k) % 4], spec_im[(3 - k) % 4]
        for g in range(3):
            re = jnp.where(group == g, spec_re[(g - k) % 4], re)
            im = jnp.where(group == g, spec_im[(g - k) % 4], im)
        re, im = re * weight, im * weight
        pieces = []
        for pair in range(nwin // 2):
            re_p, im_p = re[pair * 8 : pair * 8 + 8], im[pair * 8 : pair * 8 + 8]
            pieces.append(jnp.where(upper, re_p, pltpu.roll(im_p, 4, 0)))
            pieces.append(jnp.where(upper, pltpu.roll(re_p, 4, 0), im_p))
        pieces.append(re[top : top + 16])
        pieces.append(im[top : top + 16])
        slabs[k] = jnp.concatenate(pieces, axis=0).astype(jnp.bfloat16)
    zbuf[z] = slabs[z]

    def z_copy(r):
        return pltpu.make_async_remote_copy(
            src_ref=slabs.at[(z + r) % 4], dst_ref=zbuf.at[z],
            send_sem=z_send.at[r - 1], recv_sem=z_recv.at[r - 1],
            device_id=(chan, (z + r) % 4, win), device_id_type=MESH,
        )

    used = pl.ds(0, nwin * 8)

    def plane_copy(d, r):
        slot = (z + 4 - r) % 4
        return pltpu.make_async_remote_copy(
            src_ref=zbuf.at[slot, used], dst_ref=gath.at[d, slot],
            send_sem=p_send.at[d, r], recv_sem=p_recv.at[d, r],
            device_id=(flip(chan, d), z, win), device_id_type=MESH,
        )

    def relay_copy(d, r):
        slot = (z + 4 - r) % 4
        return pltpu.make_async_remote_copy(
            src_ref=gath.at[d, slot], dst_ref=gath.at[d + 1, slot],
            send_sem=p_send.at[d + 1, r], recv_sem=p_recv.at[d + 1, r],
            device_id=(flip(chan, 1), z, win), device_id_type=MESH,
        )

    pl.semaphore_wait(barrier, 3 + len(DIRECT))
    for r in (1, 3, 2):
        z_copy(r).start()
    for d in (6, 2, 4, 1):
        plane_copy(d, 0).start()
    last = None
    for r in (1, 3, 2):
        z_copy(r).wait_recv()
        for d in (6, 2, 4, 1):
            plane_copy(d, r).start()

    for a in range(4):
        tail = zbuf[a, top * 2 : top * 2 + 32].astype(jnp.float32) * scale
        for w in range(nwin):
            re_a = jnp.broadcast_to(tail[w : w + 1], (8, LANES))
            im_a = jnp.broadcast_to(tail[16 + w : 17 + w], (8, LANES))
            coef[0, a, w] = jnp.where(upper, re_a, im_a)
            coef[1, a, w] = jnp.where(upper, im_a, -re_a)

    for r in (0, 1, 3, 2):
        for d in (2, 4, 6):
            plane_copy(d, r).wait_recv()
            relay_copy(d, r).start()

    def block(read, first):
        def pair_step(pair, carry):
            b0 = read(pair * 2).astype(jnp.float32).reshape(nwin, 8, LANES)
            b1 = read(pair * 2 + 1).astype(jnp.float32).reshape(nwin, 8, LANES)
            for o in range(2):
                for a in range(4):
                    c = coef[o, a]
                    p0 = jnp.sum(c * b0, axis=0)
                    p1 = jnp.sum(c * b1, axis=0)
                    p0 = p0 + pltpu.roll(p0, 4, 0)
                    p1 = p1 + pltpu.roll(p1, 4, 0)
                    start = pl.multiple_of(first + pair * 8, 8)
                    res[o, a, pl.ds(start, 8), :] = jnp.where(upper, p0, p1)
            return carry

        lax.fori_loop(0, 2, pair_step, 0)

    block(lambda k: zbuf[k, 0 : nwin * 8], chan * 16)
    for d in (2, 4, 6, 1, 3, 5, 7):
        if d not in DIRECT:
            for r in range(4):
                relay_copy(d - 1, r).wait_recv()
        elif d == 1:
            for r in range(4):
                plane_copy(d, r).wait_recv()
        block(lambda k, d=d: gath[d, k], flip(chan, d) * 16)

    for o in range(2):
        for a in range(4):
            turned = res[o, a].T
            for g in range(4):
                out_ref[o, :, (g + 4 - z) % 4, a, :] = turned[g * 32 : (g + 1) * 32]

    for r in (1, 2, 3):
        z_copy(r).wait_send()
    for r in range(4):
        for d in DIRECT:
            plane_copy(d, r).wait_send()
        for d in (2, 4, 6):
            relay_copy(d, r).wait_send()


def fused_body(rec_block, rec_partner, flag_block, flag_partner):
    nwin, _, samples = rec_block.shape
    depth = -(-samples // 4 // LANES) * LANES
    basis = jnp.asarray(basis_table(samples, depth))
    vmem = pl.BlockSpec(memory_space=pltpu.VMEM)
    hbm = pl.BlockSpec(memory_space=pl.ANY)
    rows = nwin * 4 + 16
    out = pl.pallas_call(
        functools.partial(kernel, samples, 1.0 / math.sqrt(nwin)),
        out_shape=jax.ShapeDtypeStruct((2, 32, 4, 4, LANES), jnp.float32),
        in_specs=[hbm, hbm, vmem, vmem, hbm],
        out_specs=vmem,
        scratch_shapes=[
            pltpu.VMEM((nwin, samples), jnp.bfloat16),
            pltpu.VMEM((nwin, 4, samples), jnp.bfloat16),
            pltpu.VMEM((depth, 2 * F), jnp.bfloat16),
            pltpu.VMEM((rows, samples // LANES * LANES + 2 * LANES), jnp.float32),
            pltpu.VMEM((4, nwin * 8 + 32, LANES), jnp.bfloat16),
            pltpu.VMEM((4, nwin * 8 + 32, LANES), jnp.bfloat16),
            pltpu.VMEM((8, 4, nwin * 8, LANES), jnp.bfloat16),
            pltpu.VMEM((2, 4, nwin, 8, LANES), jnp.float32),
            pltpu.VMEM((2, 4, LANES, LANES), jnp.float32),
            pltpu.SemaphoreType.DMA((2,)),
            pltpu.SemaphoreType.DMA,
            pltpu.SemaphoreType.DMA((3,)),
            pltpu.SemaphoreType.DMA((3,)),
            pltpu.SemaphoreType.DMA((8, 4)),
            pltpu.SemaphoreType.DMA((8, 4)),
        ],
        compiler_params=pltpu.CompilerParams(
            collective_id=0, has_side_effects=True, vmem_limit_bytes=60 * 1024 * 1024
        ),
    )(
        rec_block.reshape(nwin, samples),
        rec_partner,
        flag_block.T,
        flag_partner.T,
        basis,
    )
    return out.reshape(2, LANES, 4, LANES)


def solution(mesh):
    placed = (
        P("win", ("chan", "freq"), None),
        P("win", ("chan", "freq"), None),
        P("win", ("chan", "freq")),
        P("win", ("chan", "freq")),
    )
    small = dict(mesh.shape) == {"chan": 8, "freq": 4, "win": 1}
    return jax.shard_map(
        fused_body if small else body,
        mesh=mesh,
        in_specs=placed,
        out_specs=P(None, "freq", "chan", "win"),
        check_vma=False,
    )
```

```python
import functools
import math

import jax
import jax.numpy as jnp
import ml_dtypes
import numpy as np
from jax import lax
from jax.experimental import pallas as pl
from jax.experimental.pallas import tpu as pltpu
from jax.sharding import PartitionSpec as P

F = 512
FLO = 60


def harmonic_kernel_grid(reading_moments, spectral_slots, reading_offsets):
    cycle_offset = reading_moments[:, None] * spectral_slots[None, :] % reading_offsets
    cycle_radians = cycle_offset.astype(jnp.float32) * (2.0 * math.pi / reading_offsets)
    return jnp.concatenate([jnp.cos(cycle_radians), -jnp.sin(cycle_radians)], axis=1).astype(
        jnp.bfloat16
    )


def transform(records):
    reading_offsets = records.shape[1]
    extent_count = reading_offsets // 4
    spectral_slots = jnp.arange(F, dtype=jnp.int32) + FLO
    accumulated = jnp.zeros((records.shape[0], 2 * F), jnp.float32)
    for cosine_lag in range(4):
        reading_moments = jnp.arange(extent_count, dtype=jnp.int32) + cosine_lag * extent_count
        harmonic_operator = harmonic_kernel_grid(reading_moments, spectral_slots, reading_offsets)
        accumulated = accumulated + jnp.dot(
            records[:, cosine_lag * extent_count : (cosine_lag + 1) * extent_count],
            harmonic_operator,
            preferred_element_type=jnp.float32,
        )
    return accumulated


def rotate(whitened):
    turned = jnp.concatenate([whitened[:, 1:2], -whitened[:, 0:1]], axis=1)
    return jnp.stack([whitened, turned])


def body(rec_block, rec_partner, flag_block, flag_partner):
    windows, block_dev, reading_offsets = rec_block.shape
    partner_dev = rec_partner.shape[1]
    channels = block_dev + partner_dev
    records = jnp.concatenate([rec_block, rec_partner], axis=1).reshape(
        windows * channels, reading_offsets
    )
    spectra = transform(records).reshape(windows, channels, 2, F)
    band_power = jnp.sum(spectra * spectra, axis=(2, 3), keepdims=True) / F
    quality = jnp.concatenate([flag_block, flag_partner], axis=1).astype(jnp.float32)[
        :, :, None, None
    ]
    whitened = (quality * spectra * lax.rsqrt(band_power + 1e-06)).astype(jnp.bfloat16)
    whitened = jnp.transpose(whitened, (0, 2, 1, 3))
    block_white = whitened[:, :, :block_dev]
    partner_white = whitened[:, :, block_dev:]
    block_white, partner_white = (
        lax.all_to_all(block_white, "freq", split_axis=3, concat_axis=2, tiled=True),
        lax.all_to_all(partner_white, "freq", split_axis=3, concat_axis=2, tiled=True),
    )
    stack_scale = 1.0 / math.sqrt(windows * lax.axis_size("win"))
    paired = rotate(block_white)
    partials = jnp.einsum(
        "owsaf,wsbf->ofab",
        paired,
        lax.all_gather(partner_white, "chan", axis=2, tiled=True),
        preferred_element_type=jnp.float32,
    )
    summed = lax.psum_scatter(partials, "win", scatter_dimension=3, tiled=True)
    return summed * stack_scale


MESH = pl.DeviceIdType.MESH
LANES = 128
ORDER = (0, 1, 3, 2)
DIRECT = (1, 2, 4, 6)


def basis_table(samples, depth):
    r = np.arange(samples // 4, dtype=np.int64)[:, None]
    lane = np.arange(LANES)
    table = np.zeros((depth, 4, 2, LANES), np.float64)
    for m in range(4):
        slab = (lane // 32 - m) % 4
        k = FLO + slab * LANES + 4 * (lane % 32) + (m - FLO) % 4
        phase = (r * k[None, :] % samples).astype(np.float64) * (2.0 * np.pi / samples)
        table[: samples // 4, m, 0] = np.cos(phase)
        table[: samples // 4, m, 1] = -np.sin(phase)
    return table.reshape(depth, 8 * LANES).astype(ml_dtypes.bfloat16)


def split(value):
    high = value.astype(jnp.bfloat16)
    return high, (value - high.astype(jnp.float32)).astype(jnp.bfloat16)


def flip(chan, d):
    core, x, y = chan % 2, (chan // 2) % 2, chan // 4
    core = 1 - core if d & 1 else core
    x = 1 - x if d & 2 else x
    y = 1 - y if d & 4 else y
    return core + 2 * x + 4 * y


def kernel(
    samples, scale,
    blk_hbm, par_hbm, fb_ref, fp_ref, basis_hbm, out_ref,
    blk, par, basis, xs, slabs, zbuf, gath, coef, res,
    load_sem, basis_sem, z_send, z_recv, p_send, p_recv,
):
    chan, z, win = lax.axis_index("chan"), lax.axis_index("freq"), lax.axis_index("win")
    nwin = blk.shape[0]

    blk_in = pltpu.make_async_copy(blk_hbm, blk, load_sem.at[0])
    par_in = pltpu.make_async_copy(par_hbm, par, load_sem.at[1])
    blk_in.start()
    par_in.start()
    basis_in = pltpu.make_async_copy(basis_hbm, basis, basis_sem)
    basis_in.start()

    barrier = pltpu.get_barrier_semaphore()
    for r in (1, 2, 3):
        pl.semaphore_signal(barrier, inc=1, device_id=(chan, (z + r) % 4, win), device_id_type=MESH)
    for d in DIRECT:
        pl.semaphore_signal(barrier, inc=1, device_id=(flip(chan, d), z, win), device_id_type=MESH)

    rows = xs.shape[0]
    top = nwin * 4
    edge = samples // LANES * LANES
    xs[:, edge:] = jnp.zeros((rows, xs.shape[1] - edge), jnp.float32)
    xs[top + nwin :, :] = jnp.zeros((rows - top - nwin, xs.shape[1]), jnp.float32)
    par_in.wait()
    for w in range(nwin):
        xs[w * 4 : w * 4 + 4, 0:samples] = par[w].astype(jnp.float32)
    blk_in.wait()
    xs[top : top + nwin, 0:samples] = blk[...].astype(jnp.float32)

    quarter, depth = samples // 4, basis.shape[0]
    x0, x1, x2, x3 = (xs[:, q * quarter : q * quarter + depth] for q in range(4))
    even, odd = x0 + x2, x1 + x3
    a_hi, a_lo = split(x0 - x2)
    b_hi, b_lo = split(x1 - x3)
    sum_hi, sum_lo = split(even + odd)
    alt_hi, alt_lo = split(even - odd)
    basis_in.wait()

    def transform_rows(parts, m):
        return jnp.dot(
            jnp.concatenate(parts, axis=0),
            basis[:, m * 2 * LANES : (m + 1) * 2 * LANES],
            preferred_element_type=jnp.float32,
        )

    spec_re, spec_im = [], []
    for m in range(4):
        if m % 2 == 0:
            got = transform_rows([sum_hi, sum_lo] if m == 0 else [alt_hi, alt_lo], m)
            got = got[:rows] + got[rows:]
            re, im = got[:, :LANES], got[:, LANES:]
        else:
            got = transform_rows([a_hi, a_lo, b_hi, b_lo], m)
            a = got[:rows] + got[rows : 2 * rows]
            b = got[2 * rows : 3 * rows] + got[3 * rows :]
            sign = 1.0 if m == 1 else -1.0
            re = a[:, :LANES] + sign * b[:, LANES:]
            im = a[:, LANES:] - sign * b[:, :LANES]
        spec_re.append(re)
        spec_im.append(im)

    power = sum(re * re + im * im for re, im in zip(spec_re, spec_im))
    power = jnp.sum(power, axis=1, keepdims=True) * (1.0 / F)
    row = lax.broadcasted_iota(jnp.int32, (rows, nwin), 0)
    lane = lax.broadcasted_iota(jnp.int32, (rows, nwin), 1)
    flags = jnp.concatenate(
        [fp_ref[...].astype(jnp.float32)] * nwin
        + [jnp.broadcast_to(fb_ref[...].astype(jnp.float32), (rows - top, nwin))],
        axis=0,
    )
    window = jnp.where(row < top, row // 4, row - top)
    quality = jnp.sum(jnp.where(lane == window, flags, 0.0), axis=1, keepdims=True)
    weight = quality * lax.rsqrt(power + 1e-06)

    upper = lax.broadcasted_iota(jnp.int32, (8, LANES), 0) < 4
    group = lax.broadcasted_iota(jnp.int32, (rows, LANES), 1) // 32
    for k in range(4):
        re, im = spec_re[(3 - k) % 4], spec_im[(3 - k) % 4]
        for g in range(3):
            re = jnp.where(group == g, spec_re[(g - k) % 4], re)
            im = jnp.where(group == g, spec_im[(g - k) % 4], im)
        re, im = re * weight, im * weight
        pieces = []
        for pair in range(nwin // 2):
            re_p, im_p = re[pair * 8 : pair * 8 + 8], im[pair * 8 : pair * 8 + 8]
            pieces.append(jnp.where(upper, re_p, pltpu.roll(im_p, 4, 0)))
            pieces.append(jnp.where(upper, pltpu.roll(re_p, 4, 0), im_p))
        pieces.append(re[top : top + 16])
        pieces.append(im[top : top + 16])
        slabs[k] = jnp.concatenate(pieces, axis=0).astype(jnp.bfloat16)
    zbuf[z] = slabs[z]

    def z_copy(r):
        return pltpu.make_async_remote_copy(
            src_ref=slabs.at[(z + r) % 4], dst_ref=zbuf.at[z],
            send_sem=z_send.at[r - 1], recv_sem=z_recv.at[r - 1],
            device_id=(chan, (z + r) % 4, win), device_id_type=MESH,
        )

    used = pl.ds(0, nwin * 8)

    def plane_copy(d, r):
        slot = (z + 4 - r) % 4
        return pltpu.make_async_remote_copy(
            src_ref=zbuf.at[slot, used], dst_ref=gath.at[d, slot],
            send_sem=p_send.at[d, r], recv_sem=p_recv.at[d, r],
            device_id=(flip(chan, d), z, win), device_id_type=MESH,
        )

    def relay_copy(d, r):
        slot = (z + 4 - r) % 4
        return pltpu.make_async_remote_copy(
            src_ref=gath.at[d, slot], dst_ref=gath.at[d + 1, slot],
            send_sem=p_send.at[d + 1, r], recv_sem=p_recv.at[d + 1, r],
            device_id=(flip(chan, 1), z, win), device_id_type=MESH,
        )

    pl.semaphore_wait(barrier, 3 + len(DIRECT))
    for r in ORDER[1:]:
        z_copy(r).start()
    for d in (6, 2, 4, 1):
        plane_copy(d, 0).start()
    for r in ORDER[1:]:
        z_copy(r).wait_recv()
        for d in (6, 2, 4, 1):
            plane_copy(d, r).start()

    def relay(r):
        for d in (2, 4, 6):
            plane_copy(d, r).wait_recv()
            relay_copy(d, r).start()

    relay(0)

    for a in range(4):
        tail = zbuf[a, top * 2 : top * 2 + 32].astype(jnp.float32) * scale
        for w in range(nwin):
            re_a = jnp.broadcast_to(tail[w : w + 1], (8, LANES))
            im_a = jnp.broadcast_to(tail[16 + w : 17 + w], (8, LANES))
            coef[0, a, w] = jnp.where(upper, re_a, im_a)
            coef[1, a, w] = jnp.where(upper, im_a, -re_a)

    half = lax.broadcasted_iota(jnp.int32, (8, LANES), 0) // 4

    def piece(data, d, r):
        slot = (z + 4 - r) % 4
        b = data.astype(jnp.float32).reshape(nwin, 8, LANES)
        start = pl.multiple_of(flip(chan, d) * 16 + slot // 2 * 8, 8)
        mine = half == slot % 2
        for o in range(2):
            for a in range(4):
                p = jnp.sum(coef[o, a] * b, axis=0)
                p = p + pltpu.roll(p, 4, 0)
                old = res[o, a, pl.ds(start, 8), :]
                res[o, a, pl.ds(start, 8), :] = jnp.where(mine, p, old)

    def held(d, r):
        return gath[d, (z + 4 - r) % 4]

    for r in range(4):
        if r:
            relay(ORDER[r])
        piece(zbuf[(z + 4 - ORDER[r]) % 4, 0 : nwin * 8], 0, ORDER[r])
        plane_copy(1, ORDER[r]).wait_recv()
        piece(held(1, ORDER[r]), 1, ORDER[r])
        for d in (2, 4, 6):
            piece(held(d, ORDER[r]), d, ORDER[r])
        if r:
            for d in (2, 4, 6):
                relay_copy(d, ORDER[r - 1]).wait_recv()
                piece(held(d + 1, ORDER[r - 1]), d + 1, ORDER[r - 1])
    for d in (2, 4, 6):
        relay_copy(d, ORDER[3]).wait_recv()
        piece(held(d + 1, ORDER[3]), d + 1, ORDER[3])

    for o in range(2):
        for a in range(4):
            turned = res[o, a].T
            for g in range(4):
                out_ref[o, :, (g + 4 - z) % 4, a, :] = turned[g * 32 : (g + 1) * 32]

    for r in (1, 2, 3):
        z_copy(r).wait_send()
    for r in range(4):
        for d in DIRECT:
            plane_copy(d, r).wait_send()
        for d in (2, 4, 6):
            relay_copy(d, r).wait_send()


def fused_body(rec_block, rec_partner, flag_block, flag_partner):
    nwin, _, samples = rec_block.shape
    depth = -(-samples // 4 // LANES) * LANES
    basis = jnp.asarray(basis_table(samples, depth))
    vmem = pl.BlockSpec(memory_space=pltpu.VMEM)
    hbm = pl.BlockSpec(memory_space=pl.ANY)
    rows = nwin * 4 + 16
    out = pl.pallas_call(
        functools.partial(kernel, samples, 1.0 / math.sqrt(nwin)),
        out_shape=jax.ShapeDtypeStruct((2, 32, 4, 4, LANES), jnp.float32),
        in_specs=[hbm, hbm, vmem, vmem, hbm],
        out_specs=vmem,
        scratch_shapes=[
            pltpu.VMEM((nwin, samples), jnp.bfloat16),
            pltpu.VMEM((nwin, 4, samples), jnp.bfloat16),
            pltpu.VMEM((depth, 2 * F), jnp.bfloat16),
            pltpu.VMEM((rows, samples // LANES * LANES + 2 * LANES), jnp.float32),
            pltpu.VMEM((4, nwin * 8 + 32, LANES), jnp.bfloat16),
            pltpu.VMEM((4, nwin * 8 + 32, LANES), jnp.bfloat16),
            pltpu.VMEM((8, 4, nwin * 8, LANES), jnp.bfloat16),
            pltpu.VMEM((2, 4, nwin, 8, LANES), jnp.float32),
            pltpu.VMEM((2, 4, LANES, LANES), jnp.float32),
            pltpu.SemaphoreType.DMA((2,)),
            pltpu.SemaphoreType.DMA,
            pltpu.SemaphoreType.DMA((3,)),
            pltpu.SemaphoreType.DMA((3,)),
            pltpu.SemaphoreType.DMA((8, 4)),
            pltpu.SemaphoreType.DMA((8, 4)),
        ],
        compiler_params=pltpu.CompilerParams(
            collective_id=0, has_side_effects=True, vmem_limit_bytes=60 * 1024 * 1024
        ),
    )(
        rec_block.reshape(nwin, samples),
        rec_partner,
        flag_block.T,
        flag_partner.T,
        basis,
    )
    return out.reshape(2, LANES, 4, LANES)


def solution(mesh):
    placed = (
        P("win", ("chan", "freq"), None),
        P("win", ("chan", "freq"), None),
        P("win", ("chan", "freq")),
        P("win", ("chan", "freq")),
    )
    small = dict(mesh.shape) == {"chan": 8, "freq": 4, "win": 1}
    return jax.shard_map(
        fused_body if small else body,
        mesh=mesh,
        in_specs=placed,
        out_specs=P(None, "freq", "chan", "win"),
        check_vma=False,
    )
```

```python
import functools
import math

import jax
import jax.numpy as jnp
import ml_dtypes
import numpy as np
from jax import lax
from jax.experimental import pallas as pl
from jax.experimental.pallas import tpu as pltpu
from jax.sharding import PartitionSpec as P

F = 512
FLO = 60


def harmonic_kernel_grid(reading_moments, spectral_slots, reading_offsets):
    cycle_offset = reading_moments[:, None] * spectral_slots[None, :] % reading_offsets
    cycle_radians = cycle_offset.astype(jnp.float32) * (2.0 * math.pi / reading_offsets)
    return jnp.concatenate([jnp.cos(cycle_radians), -jnp.sin(cycle_radians)], axis=1).astype(
        jnp.bfloat16
    )


def transform(records):
    reading_offsets = records.shape[1]
    extent_count = reading_offsets // 4
    spectral_slots = jnp.arange(F, dtype=jnp.int32) + FLO
    accumulated = jnp.zeros((records.shape[0], 2 * F), jnp.float32)
    for cosine_lag in range(4):
        reading_moments = jnp.arange(extent_count, dtype=jnp.int32) + cosine_lag * extent_count
        harmonic_operator = harmonic_kernel_grid(reading_moments, spectral_slots, reading_offsets)
        accumulated = accumulated + jnp.dot(
            records[:, cosine_lag * extent_count : (cosine_lag + 1) * extent_count],
            harmonic_operator,
            preferred_element_type=jnp.float32,
        )
    return accumulated


def rotate(whitened):
    turned = jnp.concatenate([whitened[:, 1:2], -whitened[:, 0:1]], axis=1)
    return jnp.stack([whitened, turned])


def body(rec_block, rec_partner, flag_block, flag_partner):
    windows, block_dev, reading_offsets = rec_block.shape
    partner_dev = rec_partner.shape[1]
    channels = block_dev + partner_dev
    records = jnp.concatenate([rec_block, rec_partner], axis=1).reshape(
        windows * channels, reading_offsets
    )
    spectra = transform(records).reshape(windows, channels, 2, F)
    band_power = jnp.sum(spectra * spectra, axis=(2, 3), keepdims=True) / F
    quality = jnp.concatenate([flag_block, flag_partner], axis=1).astype(jnp.float32)[
        :, :, None, None
    ]
    whitened = (quality * spectra * lax.rsqrt(band_power + 1e-06)).astype(jnp.bfloat16)
    whitened = jnp.transpose(whitened, (0, 2, 1, 3))
    block_white = whitened[:, :, :block_dev]
    partner_white = whitened[:, :, block_dev:]
    block_white, partner_white = (
        lax.all_to_all(block_white, "freq", split_axis=3, concat_axis=2, tiled=True),
        lax.all_to_all(partner_white, "freq", split_axis=3, concat_axis=2, tiled=True),
    )
    stack_scale = 1.0 / math.sqrt(windows * lax.axis_size("win"))
    paired = rotate(block_white)
    partials = jnp.einsum(
        "owsaf,wsbf->ofab",
        paired,
        lax.all_gather(partner_white, "chan", axis=2, tiled=True),
        preferred_element_type=jnp.float32,
    )
    summed = lax.psum_scatter(partials, "win", scatter_dimension=3, tiled=True)
    return summed * stack_scale


MESH = pl.DeviceIdType.MESH
LANES = 128
ORDER = (0, 1, 2, 3)
DIRECT = (1, 2, 4, 6)


def basis_table(samples, depth):
    r = np.arange(samples // 4, dtype=np.int64)[:, None]
    lane = np.arange(LANES)
    table = np.zeros((depth, 4, 2, LANES), np.float64)
    for m in range(4):
        slab = (lane // 32 - m) % 4
        k = FLO + slab * LANES + 4 * (lane % 32) + (m - FLO) % 4
        phase = (r * k[None, :] % samples).astype(np.float64) * (2.0 * np.pi / samples)
        table[: samples // 4, m, 0] = np.cos(phase)
        table[: samples // 4, m, 1] = -np.sin(phase)
    return table.reshape(depth, 8 * LANES).astype(ml_dtypes.bfloat16)


def split(value):
    high = value.astype(jnp.bfloat16)
    return high, (value - high.astype(jnp.float32)).astype(jnp.bfloat16)


def flip(chan, d):
    core, x, y = chan % 2, (chan // 2) % 2, chan // 4
    core = 1 - core if d & 1 else core
    x = 1 - x if d & 2 else x
    y = 1 - y if d & 4 else y
    return core + 2 * x + 4 * y


def across(z, r):
    low, high = z % 2, z // 2
    low = 1 - low if r & 1 else low
    high = 1 - high if r & 2 else high
    return low + 2 * high


def kernel(
    samples, scale,
    blk_hbm, par_hbm, fb_ref, fp_ref, basis_hbm, out_ref,
    blk, par, basis, xs, slabs, zbuf, gath, coef, res,
    load_sem, basis_sem, z_send, z_recv, p_send, p_recv,
):
    chan, z, win = lax.axis_index("chan"), lax.axis_index("freq"), lax.axis_index("win")
    nwin = blk.shape[0]

    blk_in = pltpu.make_async_copy(blk_hbm, blk, load_sem.at[0])
    par_in = pltpu.make_async_copy(par_hbm, par, load_sem.at[1])
    blk_in.start()
    par_in.start()
    basis_in = pltpu.make_async_copy(basis_hbm, basis, basis_sem)
    basis_in.start()

    barrier = pltpu.get_barrier_semaphore()
    for r in (1, 2, 3):
        pl.semaphore_signal(barrier, inc=1, device_id=(chan, across(z, r), win), device_id_type=MESH)
    for d in DIRECT:
        pl.semaphore_signal(barrier, inc=1, device_id=(flip(chan, d), z, win), device_id_type=MESH)

    rows = xs.shape[0]
    top = nwin * 4
    edge = samples // LANES * LANES
    xs[:, edge:] = jnp.zeros((rows, xs.shape[1] - edge), jnp.float32)
    xs[top + nwin :, :] = jnp.zeros((rows - top - nwin, xs.shape[1]), jnp.float32)
    par_in.wait()
    for w in range(nwin):
        xs[w * 4 : w * 4 + 4, 0:samples] = par[w].astype(jnp.float32)
    blk_in.wait()
    xs[top : top + nwin, 0:samples] = blk[...].astype(jnp.float32)

    quarter, depth = samples // 4, basis.shape[0]
    x0, x1, x2, x3 = (xs[:, q * quarter : q * quarter + depth] for q in range(4))
    even, odd = x0 + x2, x1 + x3
    a_hi, a_lo = split(x0 - x2)
    b_hi, b_lo = split(x1 - x3)
    sum_hi, sum_lo = split(even + odd)
    alt_hi, alt_lo = split(even - odd)
    basis_in.wait()

    def transform_rows(parts, m):
        return jnp.dot(
            jnp.concatenate(parts, axis=0),
            basis[:, m * 2 * LANES : (m + 1) * 2 * LANES],
            preferred_element_type=jnp.float32,
        )

    spec_re, spec_im = [], []
    for m in range(4):
        if m % 2 == 0:
            got = transform_rows([sum_hi, sum_lo] if m == 0 else [alt_hi, alt_lo], m)
            got = got[:rows] + got[rows:]
            re, im = got[:, :LANES], got[:, LANES:]
        else:
            got = transform_rows([a_hi, a_lo, b_hi, b_lo], m)
            a = got[:rows] + got[rows : 2 * rows]
            b = got[2 * rows : 3 * rows] + got[3 * rows :]
            sign = 1.0 if m == 1 else -1.0
            re = a[:, :LANES] + sign * b[:, LANES:]
            im = a[:, LANES:] - sign * b[:, :LANES]
        spec_re.append(re)
        spec_im.append(im)

    power = sum(re * re + im * im for re, im in zip(spec_re, spec_im))
    power = jnp.sum(power, axis=1, keepdims=True) * (1.0 / F)
    row = lax.broadcasted_iota(jnp.int32, (rows, nwin), 0)
    lane = lax.broadcasted_iota(jnp.int32, (rows, nwin), 1)
    flags = jnp.concatenate(
        [fp_ref[...].astype(jnp.float32)] * nwin
        + [jnp.broadcast_to(fb_ref[...].astype(jnp.float32), (rows - top, nwin))],
        axis=0,
    )
    window = jnp.where(row < top, row // 4, row - top)
    quality = jnp.sum(jnp.where(lane == window, flags, 0.0), axis=1, keepdims=True)
    weight = quality * lax.rsqrt(power + 1e-06)

    upper = lax.broadcasted_iota(jnp.int32, (8, LANES), 0) < 4
    group = lax.broadcasted_iota(jnp.int32, (rows, LANES), 1) // 32
    for k in range(4):
        re, im = spec_re[(3 - k) % 4], spec_im[(3 - k) % 4]
        for g in range(3):
            re = jnp.where(group == g, spec_re[(g - k) % 4], re)
            im = jnp.where(group == g, spec_im[(g - k) % 4], im)
        re, im = re * weight, im * weight
        pieces = []
        for pair in range(nwin // 2):
            re_p, im_p = re[pair * 8 : pair * 8 + 8], im[pair * 8 : pair * 8 + 8]
            pieces.append(jnp.where(upper, re_p, pltpu.roll(im_p, 4, 0)))
            pieces.append(jnp.where(upper, pltpu.roll(re_p, 4, 0), im_p))
        pieces.append(re[top : top + 16])
        pieces.append(im[top : top + 16])
        slabs[k] = jnp.concatenate(pieces, axis=0).astype(jnp.bfloat16)
    zbuf[z] = slabs[z]

    def z_copy(r):
        return pltpu.make_async_remote_copy(
            src_ref=slabs.at[across(z, r)], dst_ref=zbuf.at[z],
            send_sem=z_send.at[r - 1], recv_sem=z_recv.at[r - 1],
            device_id=(chan, across(z, r), win), device_id_type=MESH,
        )

    used = pl.ds(0, nwin * 8)

    def plane_copy(d, r):
        slot = across(z, r)
        return pltpu.make_async_remote_copy(
            src_ref=zbuf.at[slot, used], dst_ref=gath.at[d, slot],
            send_sem=p_send.at[d, r], recv_sem=p_recv.at[d, r],
            device_id=(flip(chan, d), z, win), device_id_type=MESH,
        )

    def relay_copy(d, r):
        slot = across(z, r)
        return pltpu.make_async_remote_copy(
            src_ref=gath.at[d, slot], dst_ref=gath.at[d + 1, slot],
            send_sem=p_send.at[d + 1, r], recv_sem=p_recv.at[d + 1, r],
            device_id=(flip(chan, 1), z, win), device_id_type=MESH,
        )

    pl.semaphore_wait(barrier, 3 + len(DIRECT))
    for r in ORDER[1:]:
        z_copy(r).start()
    for d in (6, 2, 4, 1):
        plane_copy(d, 0).start()
    for r in ORDER[1:]:
        z_copy(r).wait_recv()
        for d in (6, 2, 4, 1):
            plane_copy(d, r).start()

    def relay(r):
        for d in (2, 4, 6):
            plane_copy(d, r).wait_recv()
            relay_copy(d, r).start()

    relay(0)

    for a in range(4):
        tail = zbuf[a, top * 2 : top * 2 + 32].astype(jnp.float32) * scale
        for w in range(nwin):
            re_a = jnp.broadcast_to(tail[w : w + 1], (8, LANES))
            im_a = jnp.broadcast_to(tail[16 + w : 17 + w], (8, LANES))
            coef[0, a, w] = jnp.where(upper, re_a, im_a)
            coef[1, a, w] = jnp.where(upper, im_a, -re_a)

    half = lax.broadcasted_iota(jnp.int32, (8, LANES), 0) // 4

    def piece(data, d, r):
        slot = across(z, r)
        b = data.astype(jnp.float32).reshape(nwin, 8, LANES)
        start = pl.multiple_of(flip(chan, d) * 16 + slot // 2 * 8, 8)
        mine = half == slot % 2
        for o in range(2):
            for a in range(4):
                p = jnp.sum(coef[o, a] * b, axis=0)
                p = p + pltpu.roll(p, 4, 0)
                old = res[o, a, pl.ds(start, 8), :]
                res[o, a, pl.ds(start, 8), :] = jnp.where(mine, p, old)

    def held(d, r):
        return gath[d, across(z, r)]

    for r in range(4):
        if r:
            relay(ORDER[r])
        piece(zbuf[across(z, ORDER[r]), 0 : nwin * 8], 0, ORDER[r])
        plane_copy(1, ORDER[r]).wait_recv()
        piece(held(1, ORDER[r]), 1, ORDER[r])
        for d in (2, 4, 6):
            piece(held(d, ORDER[r]), d, ORDER[r])
        if r:
            for d in (2, 4, 6):
                relay_copy(d, ORDER[r - 1]).wait_recv()
                piece(held(d + 1, ORDER[r - 1]), d + 1, ORDER[r - 1])
    for d in (2, 4, 6):
        relay_copy(d, ORDER[3]).wait_recv()
        piece(held(d + 1, ORDER[3]), d + 1, ORDER[3])

    for o in range(2):
        for a in range(4):
            turned = res[o, a].T
            for g in range(4):
                out_ref[o, :, (g + 4 - z) % 4, a, :] = turned[g * 32 : (g + 1) * 32]

    for r in (1, 2, 3):
        z_copy(r).wait_send()
    for r in range(4):
        for d in DIRECT:
            plane_copy(d, r).wait_send()
        for d in (2, 4, 6):
            relay_copy(d, r).wait_send()


def fused_body(rec_block, rec_partner, flag_block, flag_partner):
    nwin, _, samples = rec_block.shape
    depth = -(-samples // 4 // LANES) * LANES
    basis = jnp.asarray(basis_table(samples, depth))
    vmem = pl.BlockSpec(memory_space=pltpu.VMEM)
    hbm = pl.BlockSpec(memory_space=pl.ANY)
    rows = nwin * 4 + 16
    out = pl.pallas_call(
        functools.partial(kernel, samples, 1.0 / math.sqrt(nwin)),
        out_shape=jax.ShapeDtypeStruct((2, 32, 4, 4, LANES), jnp.float32),
        in_specs=[hbm, hbm, vmem, vmem, hbm],
        out_specs=vmem,
        scratch_shapes=[
            pltpu.VMEM((nwin, samples), jnp.bfloat16),
            pltpu.VMEM((nwin, 4, samples), jnp.bfloat16),
            pltpu.VMEM((depth, 2 * F), jnp.bfloat16),
            pltpu.VMEM((rows, samples // LANES * LANES + 2 * LANES), jnp.float32),
            pltpu.VMEM((4, nwin * 8 + 32, LANES), jnp.bfloat16),
            pltpu.VMEM((4, nwin * 8 + 32, LANES), jnp.bfloat16),
            pltpu.VMEM((8, 4, nwin * 8, LANES), jnp.bfloat16),
            pltpu.VMEM((2, 4, nwin, 8, LANES), jnp.float32),
            pltpu.VMEM((2, 4, LANES, LANES), jnp.float32),
            pltpu.SemaphoreType.DMA((2,)),
            pltpu.SemaphoreType.DMA,
            pltpu.SemaphoreType.DMA((3,)),
            pltpu.SemaphoreType.DMA((3,)),
            pltpu.SemaphoreType.DMA((8, 4)),
            pltpu.SemaphoreType.DMA((8, 4)),
        ],
        compiler_params=pltpu.CompilerParams(
            collective_id=0, has_side_effects=True, vmem_limit_bytes=60 * 1024 * 1024
        ),
    )(
        rec_block.reshape(nwin, samples),
        rec_partner,
        flag_block.T,
        flag_partner.T,
        basis,
    )
    return out.reshape(2, LANES, 4, LANES)


def solution(mesh):
    placed = (
        P("win", ("chan", "freq"), None),
        P("win", ("chan", "freq"), None),
        P("win", ("chan", "freq")),
        P("win", ("chan", "freq")),
    )
    small = dict(mesh.shape) == {"chan": 8, "freq": 4, "win": 1}
    return jax.shard_map(
        fused_body if small else body,
        mesh=mesh,
        in_specs=placed,
        out_specs=P(None, "freq", "chan", "win"),
        check_vma=False,
    )
```
